32 devices in a mesh: dp: 8 (over z, core), expert: 4 (over y, x).
Axes of the slice: x: 2, y: 2, z: 4, core: 2. Of those that a mesh axis runs over, the one named last changes fastest.
Arguments:
- tokens: bfloat16 [6144, 4096], P(('dp', 'expert')), may hold values from -24 to 24
- routes: int32 [6144, 2], P(('dp', 'expert')), may hold values from 0 to 3, all different within a row; in each aligned block of 192 rows (0 to 191, 192 to 383, ...) at most 128 rows name the same one
- positives: int32 [64], P(('dp', 'expert')), may hold values from 0 to 63, each once
- expert_out: bfloat16 [8, 4, 4, 128, 4096], P('dp', 'expert'), may hold values from -6 to 6
- router: bfloat16 [4096, 4], replicated, may hold values from -0.09375 to 0.09375
- norm_gain: float32 [4096], replicated, may hold values from 0.25 to 1.75
- loss_scale: float32 [], replicated, may hold values from 8192 to 65536
Outputs:
- token_grad: bfloat16 [6144, 4096], P(('dp', 'expert'))
- expert_grad: bfloat16 [8, 4, 4, 128, 4096], P('dp', 'expert')
- router_grad: float32 [4096, 4], replicated
- loss: float32 [], replicated
The draws below stay inside these ranges and needn't reach their ends.
Inputs may be any that keep to these rules, and one draw needn't show every extreme that they name: `routes`: each row names 2 different experts; among the rows of one device no expert is named by more than 128 rows, a bound that some block reaches. `positives`: A permutation of the records.
All inputs are finite; a program needn't handle non-finite values.
Results may differ from the reference program's by a relative error of at most 0.0061.
Values may be sent and summed in bfloat16 or wider, within the bound.
A program may use at most 128 MiB of HBM per device.

```python
import math
import jax
import jax.numpy as jnp
import numpy as np
from jax import lax

D = 4096
TOPK = 2
PAIR_DEV = 2
SEQ = 48
EXPERTS = 4
TOK_DEV = 192
CAP = 128
PAIRS = 64
TOKENS = 6144
N_DP = 8
N_EXPERT = 4


def draw_tokens(key, part):
    base_key = jax.random.fold_in(key, 7)
    key_common, key_noise = jax.random.split(base_key, 2)
    seq_count = TOKENS // SEQ
    common = jax.random.normal(key_common, (seq_count, 1, D), jnp.float32)
    noise_rows = jax.random.normal(key_noise, (seq_count, SEQ, D), jnp.float32)
    values = jnp.clip(common + noise_rows, -24.0, 24.0)
    return values.reshape(TOKENS, D).astype(jnp.bfloat16)


def level_of(stream_key, extent, cuts, low, high):
    def one(position, shards_of):
        draws = jax.random.uniform(jax.random.fold_in(jax.random.fold_in(stream_key, 6), position), (shards_of,), jnp.float32, low / len(cuts), high / len(cuts))
        return jnp.repeat(jnp.exp(draws), extent[position] // shards_of).reshape((-1,) + (1,) * (len(extent) - position - 1))

    factor_of = one(*cuts[0])
    for cut in cuts[1:]:
        factor_of = factor_of * one(*cut)
    return factor_of


def deal_out(stream_key, own, number, rows, amount, top, reach, slope):
    ranking = jax.random.permutation(stream_key, amount)
    crowded, usual = load_shares(amount, rows * top, reach, slope, True), load_shares(amount, rows * top, reach, slope, False)
    places = jnp.arange(amount)

    def named(tallies, rotation):
        used = int((tallies > 0).sum())
        fixed = max(1, used // 4)
        passed = fixed + (places - fixed + rotation * (used - fixed)) % max(1, amount - fixed)
        return jnp.zeros((amount,), jnp.int32).at[ranking[jnp.where(places < fixed, places, passed)]].set(jnp.asarray(tallies, jnp.int32))

    tallies = jnp.where(number % 4 == 0, named(crowded, number // 4), named(usual, number - number // 4 - 1))
    mixed = jax.random.permutation(jax.random.fold_in(own, 3), amount)
    source_of, sink = mixed[0:amount // 2 * 2:2], mixed[1:amount // 2 * 2:2]
    slack = jnp.minimum(tallies[source_of] - 1, reach - tallies[sink]) // 2
    slack = jnp.where((source_of == ranking[0]) | (sink == ranking[0]) | (tallies[sink] == 0), 0, jnp.maximum(slack, 0))
    passed = jax.random.randint(jax.random.fold_in(own, 4), (amount // 2,), 0, 1 << 20) % (slack + 1)
    tallies = tallies.at[source_of].add(-passed).at[sink].add(passed)
    labels = jnp.searchsorted(jnp.cumsum(tallies), jnp.arange(rows * top), side="right").astype(jnp.int32)
    listing = labels.reshape(top, rows).T
    listing = listing[jax.random.permutation(jax.random.fold_in(own, 1), rows)]
    rotation = jax.random.randint(jax.random.fold_in(own, 2), (rows, 1), 0, top)
    return jnp.take_along_axis(listing, (jnp.arange(top)[None, :] + rotation) % top, axis=1)


def load_shares(count, total, most, skew, full):
    portions = [(1 << 20) // math.isqrt(standing ** skew) + 1 for standing in range(1, count + 1)]
    largest = most if full else min(most, max(-(-total // count), total * portions[0] // sum(portions)))
    least = 1 if total - largest >= count - 1 else 0
    counts, spare = [largest] + [least] * (count - 1), total - largest - least * (count - 1)
    while spare > 0:
        candidates = [i for i in range(1, count) if counts[i] < largest] or [i for i in range(1, count) if counts[i] < most]
        whole, budget = sum([portions[i] for i in candidates]), spare
        for i in candidates:
            more = min(most - counts[i], max(1, budget * portions[i] // whole), spare)
            counts[i] = counts[i] + more
            spare = spare - more
    return np.array(counts)


def normal_values(rng, dims, deviation, most, shards=(), kind=jnp.bfloat16):
    array = deviation * jax.random.normal(rng, dims, jnp.float32)
    if shards:
        array = array * level_of(rng, dims, shards, -0.22, 0.18)
    return jnp.clip(array, -most, most).astype(kind)


def setup_inputs(seed: int = 0) -> dict:
    keys = jax.random.split(jax.random.key(seed), 8)
    tokens = draw_tokens(jax.random.fold_in(keys[7], 71), 0)
    routes_keys = jax.random.split(jax.random.fold_in(keys[1], 1), TOKENS // TOK_DEV)
    routes_turns = jax.random.permutation(jax.random.fold_in(keys[1], 3), TOKENS // TOK_DEV)
    routes = jax.vmap(lambda own, number: deal_out(jax.random.fold_in(keys[1], 2), own, number, TOK_DEV, EXPERTS, TOPK, CAP, 1))(routes_keys, routes_turns).reshape((TOKENS, TOPK))
    positives = jax.random.permutation(keys[2], PAIRS).astype(jnp.int32)
    expert_out = normal_values(keys[3], (N_DP, EXPERTS, EXPERTS, CAP, D), 1.0, 6.0, ((0, 8), (1, 4)))
    router = normal_values(keys[4], (D, EXPERTS), D ** -0.5, 0.09375)
    norm_gain = jnp.clip(1.0 + 0.15 * jax.random.normal(keys[5], (D,), jnp.float32), 0.25, 1.75)
    loss_scale = jnp.clip(jnp.exp(jax.random.uniform(keys[6], (), jnp.float32, math.log(8192.0), math.log(65536.0))), 8192.0, 65536.0)
    return {"tokens": tokens, "routes": routes, "positives": positives, "expert_out": expert_out, "router": router, "norm_gain": norm_gain, "loss_scale": loss_scale}


norm_eps = 1e-05

def slot_where(routes, experts, capacity):
    hit_table = (routes[:, :, None] == jnp.arange(experts, dtype=jnp.int32)[None, None, :]).astype(jnp.int32)
    flat_hits = hit_table.reshape(-1, experts)
    before = jnp.cumsum(flat_hits, axis=0) - flat_hits
    slot_rank = lax.optimization_barrier(jnp.sum(before * flat_hits, axis=1)).reshape(routes.shape)
    return (routes * capacity + slot_rank).astype(jnp.int32)

def forward_rows(tokens, routes, received, router, norm_gain):
    experts = received.shape[0]
    capacity = received.shape[1]
    hidden_width = received.shape[2]
    logits = jnp.dot(tokens, router, preferred_element_type=jnp.float32)
    one_hot = (routes[:, :, None] == jnp.arange(experts, dtype=jnp.int32)[None, None, :]).astype(jnp.float32)
    chosen = lax.optimization_barrier(jnp.sum(one_hot * logits[:, None, :], axis=2))
    gate_mix = jax.nn.softmax(chosen, axis=1)
    slot_rows = slot_where(routes, experts, capacity)
    fetched = received.reshape(experts * capacity, hidden_width)[slot_rows]
    summed_rows = tokens.astype(jnp.float32) + gate_mix[:, 0:1] * fetched[:, 0].astype(jnp.float32) + gate_mix[:, 1:2] * fetched[:, 1].astype(jnp.float32)
    inverse = lax.rsqrt(lax.optimization_barrier(jnp.mean(summed_rows * summed_rows, axis=1, keepdims=True)) + norm_eps)
    normed = summed_rows * inverse * norm_gain
    pooled = lax.optimization_barrier(jnp.mean(normed.reshape(-1, SEQ, hidden_width), axis=1)).astype(jnp.bfloat16)
    return (pooled, (gate_mix, one_hot, slot_rows, fetched, summed_rows, inverse))

def backward_rows(tokens, router, norm_gain, saved, grad_pool, experts, capacity):
    gate_mix, one_hot, slot_rows, fetched, summed_rows, inverse = saved
    hidden_width = tokens.shape[1]
    grad_rows = jnp.broadcast_to(grad_pool[:, None, :] / SEQ, (grad_pool.shape[0], SEQ, hidden_width)).reshape(-1, hidden_width)
    weighted = grad_rows * norm_gain
    grad_summed = inverse * weighted - summed_rows * inverse ** 3 * lax.optimization_barrier(jnp.mean(weighted * summed_rows, axis=1, keepdims=True))
    grad_gate = lax.optimization_barrier(jnp.sum(grad_summed[:, None, :] * fetched.astype(jnp.float32), axis=2))
    grad_chosen = gate_mix * (grad_gate - lax.optimization_barrier(jnp.sum(gate_mix * grad_gate, axis=1, keepdims=True)))
    grad_logits = lax.optimization_barrier(jnp.sum(one_hot * grad_chosen[:, :, None], axis=1)).astype(jnp.bfloat16)
    router_part = lax.dot_general(tokens, grad_logits, (((0,), (0,)), ((), ())), preferred_element_type=jnp.float32)
    through_router = lax.dot_general(grad_logits, router, (((1,), (1,)), ((), ())), preferred_element_type=jnp.float32)
    token_grad = (grad_summed + through_router).astype(jnp.bfloat16)
    outgoing = (gate_mix[:, :, None] * grad_summed[:, None, :]).astype(jnp.bfloat16).reshape(-1, hidden_width)
    sendback = jnp.zeros((experts * capacity, hidden_width), jnp.bfloat16).at[slot_rows.reshape(-1)].set(outgoing)
    return (token_grad, sendback.reshape(experts, capacity, hidden_width), router_part)

def reference(tokens, routes, positives, expert_out, router, norm_gain, loss_scale):
    device_count = N_DP * N_EXPERT
    experts = expert_out.shape[1]
    capacity = expert_out.shape[3]
    hidden_width = tokens.shape[1]
    row_blocks = tokens.reshape(device_count, -1, hidden_width)
    route_blocks = routes.reshape(device_count, -1, TOPK)
    received = jnp.transpose(expert_out, (0, 2, 1, 3, 4)).reshape(device_count, experts, capacity, hidden_width)

    def embed_block(bundle):
        return forward_rows(bundle[0], bundle[1], bundle[2], router, norm_gain)[0]
    pooled = lax.map(embed_block, (row_blocks, route_blocks, received))
    queries = pooled[:, :PAIR_DEV].reshape(PAIRS, hidden_width)
    records = pooled[:, PAIR_DEV:].reshape(PAIRS, hidden_width)
    score_scale = 4.0 / math.sqrt(D)
    scores = lax.dot_general(queries, records, (((1,), (1,)), ((), ())), preferred_element_type=jnp.float32) * score_scale
    highest = lax.optimization_barrier(jnp.max(scores, axis=1, keepdims=True))
    log_total = highest[:, 0] + jnp.log(lax.optimization_barrier(jnp.sum(jnp.exp(scores - highest), axis=1)))
    is_positive = jnp.arange(PAIRS, dtype=jnp.int32)[None, :] == positives[:, None]
    positive_score = lax.optimization_barrier(jnp.sum(jnp.where(is_positive, scores, jnp.zeros_like(scores)), axis=1))
    loss = jnp.mean(log_total - positive_score)
    softmax_rows = jnp.exp(scores - log_total[:, None])
    score_grad = ((softmax_rows - is_positive.astype(jnp.float32)) * (loss_scale / PAIRS)).astype(jnp.bfloat16)
    grad_queries = jnp.dot(score_grad, records, preferred_element_type=jnp.float32) * score_scale
    grad_records = lax.dot_general(score_grad, queries, (((0,), (0,)), ((), ())), preferred_element_type=jnp.float32) * score_scale
    grad_pool = jnp.concatenate([grad_queries.reshape(device_count, PAIR_DEV, hidden_width), grad_records.reshape(device_count, PAIR_DEV, hidden_width)], axis=1)

    def back_block(bundle):
        pooled_rows, saved = forward_rows(bundle[0], bundle[1], bundle[2], router, norm_gain)
        return backward_rows(bundle[0], router, norm_gain, saved, bundle[3], experts, capacity)
    token_parts, sendback, router_parts = lax.map(back_block, (row_blocks, route_blocks, received, grad_pool))
    token_grad = token_parts.reshape(-1, hidden_width)
    expert_grad = jnp.transpose(sendback.reshape(N_DP, N_EXPERT, experts, capacity, hidden_width), (0, 2, 1, 3, 4))
    router_grad = lax.optimization_barrier(jnp.sum(router_parts, axis=0))
    return (token_grad, expert_grad, router_grad, loss)
```

```python
import functools
import math

import jax
import jax.numpy as jnp
from jax import lax
from jax.experimental import pallas as pl
from jax.experimental.pallas import tpu as pltpu
from jax.sharding import PartitionSpec as P

PAIR_DEV = 2
SEQ = 48
NORM_EPS = 1e-05
CHUNKS = 4
TILE = 512
MESH = pl.DeviceIdType.MESH
BF16, F32, I32 = jnp.bfloat16, jnp.float32, jnp.int32
NT = (((1,), (1,)), ((), ()))


def iota(shape, dim):
    return lax.broadcasted_iota(I32, shape, dim)


def dot(a, b):
    return jnp.dot(a, b, preferred_element_type=F32)


def dot_nt(a, b):
    return lax.dot_general(a, b, NT, preferred_element_type=F32)


def lane_sum(x):
    return jnp.sum(x, axis=1, keepdims=True)


def fold(x):
    total = x[:, :128]
    for i in range(1, x.shape[1] // 128):
        total = total + x[:, i * 128 : (i + 1) * 128]
    return total


def split3(x):
    hi = x.astype(BF16).astype(F32)
    mid = (x - hi).astype(BF16).astype(F32)
    return hi, mid, x - hi - mid


def log2(n):
    assert n & (n - 1) == 0
    return n.bit_length() - 1


def kernel(
    n_dp, n_ep, experts, cap,
    tok_hbm, routes_ref, pos_ref, eo_hbm, router_ref, gain_ref, scale_ref,
    tg_hbm, eg_hbm, rg_out, loss_ref,
    tok, recv, feat, summed, sq, sf, pick, pick_t, back, xrows, pay, gath, qr, ghl, tgb, rpart, rsb, exb, agb,
    tok_sem, own_sem, a_send, a_recv, z_send, z_recv, e_send, e_recv, c_send, c_recv,
    b_send, b_recv, r_send, r_recv, x_send, x_recv, g_send, g_recv, out_sem,
):
    d = lax.axis_index("dp")
    e = lax.axis_index("expert")
    rows, width = tok.shape
    slots = experts * cap
    n_z = n_dp // 2
    core, z = lax.rem(d, 2), d // 2
    pairs = PAIR_DEV * n_dp * n_ep
    wc = width // CHUNKS
    wr = width // n_dp
    ng = PAIR_DEV * n_ep
    score_scale = 4.0 / math.sqrt(width)

    def dp_peer(o):
        return lax.rem(d + o, n_dp)

    def ep_peer(o):
        return lax.rem(e + o, n_ep)

    barrier = pltpu.get_barrier_semaphore()
    for o in range(1, n_dp):
        pl.semaphore_signal(barrier, inc=1, device_id=(dp_peer(o), e), device_id_type=MESH)
    for o in range(1, n_ep):
        pl.semaphore_signal(barrier, inc=1, device_id=(d, ep_peer(o)), device_id_type=MESH)

    tok_copy = pltpu.make_async_copy(tok_hbm, tok, tok_sem.at[0])
    tok_copy.start()

    def ep_rows(i):
        return pl.ds(pl.multiple_of(i * cap, cap), cap)

    own_copy = pltpu.make_async_copy(eo_hbm.at[ep_rows(e)], recv.at[ep_rows(e)], own_sem.at[0])
    own_copy.start()
    pl.semaphore_wait(barrier, n_dp - 1 + n_ep - 1)

    a_copies = []
    for c in range(CHUNKS):
        cols = pl.ds(c * wc, wc)
        for o in range(1, n_ep):
            copy = pltpu.make_async_remote_copy(
                src_ref=eo_hbm.at[ep_rows(ep_peer(o)), cols],
                dst_ref=recv.at[ep_rows(e), cols],
                send_sem=a_send.at[c, o - 1],
                recv_sem=a_recv.at[c, o - 1],
                device_id=(d, ep_peer(o)),
                device_id_type=MESH,
            )
            copy.start()
            a_copies.append(copy)

    tok_copy.wait()
    logits = dot_nt(tok[...], router_ref[...])
    route = [routes_ref[:, 0:1], routes_ref[:, 1:2]]
    lane_e = iota((rows, 128), 1)
    lane_l = iota(logits.shape, 1)
    chosen = [lane_sum(jnp.where(lane_l == r, logits, 0.0)) for r in route]
    highest = jnp.maximum(chosen[0], chosen[1])
    expo = [jnp.exp(x - highest) for x in chosen]
    gate = [x / (expo[0] + expo[1]) for x in expo]
    hits = jnp.where((lane_e == route[0]) | (lane_e == route[1]), 1.0, 0.0).astype(BF16)
    lower = jnp.where(iota((rows, rows), 1) < iota((rows, rows), 0), 1.0, 0.0).astype(BF16)
    before = dot(lower, hits)
    column = iota((rows, slots), 1).astype(F32)
    for k in range(2):
        rank = lane_sum(jnp.where(lane_e == route[k], before, 0.0))
        slot = route[k].astype(F32) * float(cap) + rank
        one = jnp.where(column == slot, 1.0, 0.0)
        pick[k * rows : (k + 1) * rows, :] = one.astype(BF16)
        pick_t[k, :, :] = jnp.transpose(one).astype(BF16)

    sq[...] = jnp.zeros_like(sq)
    sf[...] = jnp.zeros_like(sf)
    own_copy.wait()
    for c in range(CHUNKS):
        for o in range(1, n_ep):
            a_copies[c * (n_ep - 1) + o - 1].wait_recv()

        def forward(i, _, c=c):
            cols = pl.ds(pl.multiple_of(c * wc + i * TILE, TILE), TILE)
            got = dot(pick[...], recv[:, cols])
            feat[:, cols] = got.astype(BF16)
            f0, f1 = got[:rows], got[rows:]
            s = tok[:, cols].astype(F32) + gate[0] * f0 + gate[1] * f1
            summed[:, cols] = s
            sq[...] += fold(s * s)
            sf[0, :, :] += fold(s * f0)
            sf[1, :, :] += fold(s * f1)
            return 0

        lax.fori_loop(0, wc // TILE, forward, 0)

    inverse = lax.rsqrt(lane_sum(sq[...]) * (1.0 / width) + NORM_EPS)
    for c in range(CHUNKS):
        for i in range(wc // TILE):
            cols = slice(c * wc + i * TILE, c * wc + (i + 1) * TILE)
            normed = summed[:, cols] * inverse * gain_ref[:, cols]
            for q in range(2 * PAIR_DEV):
                pay[c * 4 + q : c * 4 + q + 1, i * TILE : (i + 1) * TILE] = jnp.sum(
                    normed[q * SEQ : (q + 1) * SEQ], axis=0, keepdims=True
                ) * (1.0 / SEQ)
    tag_row, tag_lane = iota((16, 128), 0), iota((16, 128), 1)
    tags = jnp.zeros((16, 128), F32)
    for q in range(PAIR_DEV):
        p = pos_ref[q]
        high = jnp.right_shift(p, 4).astype(F32)
        low = jnp.bitwise_and(p, 15).astype(F32)
        tags = jnp.where((tag_row == q) & (tag_lane == 0), high, tags)
        tags = jnp.where((tag_row == q) & (tag_lane == 1), low, tags)
    pay[:, wc:] = tags

    def block(first, count):
        return pl.ds(pl.multiple_of(first * 16, 16), count * 16)

    mine = (core * n_ep + e) * n_z + z
    gath[block(mine, 1), :] = pay[...].astype(BF16)
    z_copies = []
    for o in range(1, n_z):
        copy = pltpu.make_async_remote_copy(
            src_ref=gath.at[block(mine, 1)],
            dst_ref=gath.at[block(mine, 1)],
            send_sem=z_send.at[o - 1],
            recv_sem=z_recv.at[o - 1],
            device_id=(dp_peer(2 * o), e),
            device_id_type=MESH,
        )
        copy.start()
        z_copies.append(copy)

    seq_of = iota((rows, 1), 0) // SEQ
    code = jnp.where(seq_of < PAIR_DEV, e * PAIR_DEV + seq_of, ng + e * PAIR_DEV + seq_of - PAIR_DEV)
    inv3 = split3(inverse)
    notes = jnp.zeros((slots, 128), F32)
    for k in range(2):
        values = list(split3(gate[k])) + list(inv3) + [code.astype(F32)]
        note = jnp.zeros((rows, 128), F32)
        for i, v in enumerate(values):
            note = jnp.where(lane_e == i, v, note)
        notes = notes + dot(pick_t[k], note.astype(BF16))
    back[:, width:] = notes.astype(BF16)

    def place(i, _):
        cols = pl.ds(pl.multiple_of(i * TILE, TILE), TILE)
        both = pick_t[0] + pick_t[1]
        back[:, cols] = dot(both, summed[:, cols].astype(BF16)).astype(BF16)
        return 0

    lax.fori_loop(0, width // TILE, place, 0)

    for copy in z_copies:
        copy.wait_recv()
    line = (core * n_ep + e) * n_z
    e_copies = []
    for o in range(1, n_ep):
        copy = pltpu.make_async_remote_copy(
            src_ref=gath.at[block(line, n_z)],
            dst_ref=gath.at[block(line, n_z)],
            send_sem=e_send.at[o - 1],
            recv_sem=e_recv.at[o - 1],
            device_id=(d, ep_peer(o)),
            device_id_type=MESH,
        )
        copy.start()
        e_copies.append(copy)
    back_own = pltpu.make_async_copy(back.at[ep_rows(e)], xrows.at[ep_rows(e)], own_sem.at[1])
    back_own.start()
    b_copies = []
    for c in range(CHUNKS):
        cols = pl.ds(c * wc, wc + (128 if c == CHUNKS - 1 else 0))
        for o in range(1, n_ep):
            copy = pltpu.make_async_remote_copy(
                src_ref=back.at[ep_rows(ep_peer(o)), cols],
                dst_ref=xrows.at[ep_rows(e), cols],
                send_sem=b_send.at[c, o - 1],
                recv_sem=b_recv.at[c, o - 1],
                device_id=(d, ep_peer(o)),
                device_id_type=MESH,
            )
            copy.start()
            b_copies.append(copy)
    for copy in e_copies:
        copy.wait_recv()
    half = core * n_ep * n_z
    c_copy = pltpu.make_async_remote_copy(
        src_ref=gath.at[block(half, n_ep * n_z)],
        dst_ref=gath.at[block(half, n_ep * n_z)],
        send_sem=c_send.at[0],
        recv_sem=c_recv.at[0],
        device_id=(d + 1 - 2 * core, e),
        device_id_type=MESH,
    )
    c_copy.start()
    c_copy.wait_recv()

    total = n_dp * n_ep * 16
    which = iota((2 * pairs, total), 0)
    source = iota((2 * pairs, total), 1)
    pair = jnp.bitwise_and(which, pairs - 1)
    is_record = jnp.right_shift(which, log2(pairs))
    blk = jnp.right_shift(pair, log2(PAIR_DEV))
    of_e = jnp.bitwise_and(blk, n_ep - 1)
    of_d = jnp.right_shift(blk, log2(n_ep))
    place_of = (jnp.bitwise_and(of_d, 1) * n_ep + of_e) * n_z + jnp.right_shift(of_d, 1)
    start = place_of * 16 + is_record * PAIR_DEV + jnp.bitwise_and(pair, PAIR_DEV - 1)
    for c in range(CHUNKS):
        take = jnp.where(source == start + c * 4, 1.0, 0.0).astype(BF16)
        if c == 0:
            tag = dot(take[:pairs], gath[:, wc:])
            positive = tag[:, 0:1] * 16.0 + tag[:, 1:2]
        qr[:, c * wc : (c + 1) * wc] = dot(take, gath[:, :wc]).astype(BF16)
    scores = dot_nt(qr[:pairs], qr[pairs:]) * score_scale
    top = jnp.max(scores, axis=1, keepdims=True)
    log_total = top + jnp.log(lane_sum(jnp.exp(scores - top)))
    is_positive = iota((pairs, pairs), 1).astype(F32) == positive
    positive_score = lane_sum(jnp.where(is_positive, scores, 0.0))
    loss = jnp.sum(log_total - positive_score, axis=0, keepdims=True) * (1.0 / pairs)
    loss_ref[...] = jnp.broadcast_to(loss, loss_ref.shape)
    score_grad = (
        (jnp.exp(scores - log_total) - jnp.where(is_positive, 1.0, 0.0)) * (scale_ref[0] * (1.0 / pairs))
    ).astype(BF16)
    group_shape = (max(16, ng), pairs)
    group = jnp.where(iota(group_shape, 1) == iota(group_shape, 0) + d * ng, 1.0, 0.0).astype(BF16)
    grad_q = dot(group, score_grad).astype(BF16)
    grad_r = dot_nt(group, score_grad).astype(BF16)

    def pooled_grads(i, _):
        cols = pl.ds(pl.multiple_of(i * TILE, TILE), TILE)
        gq = dot(grad_q, qr[pairs:, cols])[:ng]
        gr = dot(grad_r, qr[:pairs, cols])[:ng]
        g = jnp.concatenate([gq, gr], axis=0) * (score_scale / SEQ) * gain_ref[:, cols]
        hi = g.astype(BF16)
        ghl[: 2 * ng, cols] = hi
        ghl[2 * ng :, cols] = (g - hi.astype(F32)).astype(BF16)
        return 0

    lax.fori_loop(0, width // TILE, pooled_grads, 0)

    lane_g = iota((rows, 4 * ng), 1)
    mark = jnp.where((lane_g == code) | (lane_g == code + 2 * ng), 1.0, 0.0)
    own = lane_sum(mark * dot_nt(tok[...], ghl[...]))
    along = dot_nt(feat[...], ghl[...])
    a0, a1 = lane_sum(mark * along[:rows]), lane_sum(mark * along[rows:])
    mean_ws = (own + gate[0] * a0 + gate[1] * a1) * (1.0 / width)
    coef = inverse * inverse * inverse * mean_ws
    gg0 = inverse * a0 - coef * lane_sum(sf[0])
    gg1 = inverse * a1 - coef * lane_sum(sf[1])
    gg = gate[0] * gg0 + gate[1] * gg1
    grad_logits = jnp.where(lane_e == route[0], gate[0] * (gg0 - gg), 0.0) + jnp.where(
        lane_e == route[1], gate[1] * (gg1 - gg), 0.0
    )
    gl = grad_logits[:, :16].astype(BF16)
    gl_t = jnp.transpose(grad_logits)[:16].astype(BF16)
    for i in range(n_dp):
        rpart[i, :, :] = dot(gl_t, tok[:, i * wr : (i + 1) * wr])[:8]
    rsb[d] = rpart[d]
    r_copies = []
    for o in range(1, n_dp):
        copy = pltpu.make_async_remote_copy(
            src_ref=rpart.at[dp_peer(o)],
            dst_ref=rsb.at[d],
            send_sem=r_send.at[o - 1],
            recv_sem=r_recv.at[o - 1],
            device_id=(dp_peer(o), e),
            device_id_type=MESH,
        )
        copy.start()
        r_copies.append(copy)
    markb = mark.astype(BF16)

    def token_grads(i, _):
        cols = pl.ds(pl.multiple_of(i * TILE, TILE), TILE)
        w = dot(markb, ghl[:, cols])
        through = dot(gl, router_ref[:, cols])
        tgb[:, cols] = (inverse * w - coef * summed[:, cols] + through).astype(BF16)
        return 0

    lax.fori_loop(0, width // TILE, token_grads, 0)
    tg_copy = pltpu.make_async_copy(tgb, tg_hbm, out_sem.at[CHUNKS])
    tg_copy.start()

    for copy in r_copies:
        copy.wait_recv()
    part = rsb[0]
    for i in range(1, n_dp):
        part = part + rsb[i]
    exb[e] = part
    x_copies = []
    for o in range(1, n_ep):
        copy = pltpu.make_async_remote_copy(
            src_ref=exb.at[e],
            dst_ref=exb.at[e],
            send_sem=x_send.at[o - 1],
            recv_sem=x_recv.at[o - 1],
            device_id=(d, ep_peer(o)),
            device_id_type=MESH,
        )
        copy.start()
        x_copies.append(copy)

    back_own.wait()
    dots = jnp.zeros((slots, 4 * ng), F32)
    for c in range(CHUNKS):
        for o in range(1, n_ep):
            b_copies[c * (n_ep - 1) + o - 1].wait_recv()
        dots = dots + dot_nt(xrows[:, c * wc : (c + 1) * wc], ghl[:, c * wc : (c + 1) * wc])

    for copy in x_copies:
        copy.wait_recv()
    part = exb[0]
    for i in range(1, n_ep):
        part = part + exb[i]
    agb[d] = part
    g_copies = []
    for o in range(1, n_dp):
        copy = pltpu.make_async_remote_copy(
            src_ref=agb.at[d],
            dst_ref=agb.at[d],
            send_sem=g_send.at[o - 1],
            recv_sem=g_recv.at[o - 1],
            device_id=(dp_peer(o), e),
            device_id_type=MESH,
        )
        copy.start()
        g_copies.append(copy)

    note = xrows[:, width:].astype(F32)
    x_gate = note[:, 0:1] + note[:, 1:2] + note[:, 2:3]
    x_inv = note[:, 3:4] + note[:, 4:5] + note[:, 5:6]
    x_code = note[:, 6:7]
    lane_x = iota((slots, 4 * ng), 1).astype(F32)
    x_mark = jnp.where((lane_x == x_code) | (lane_x == x_code + float(2 * ng)), 1.0, 0.0)
    x_mean = lane_sum(x_mark * dots) * (1.0 / width)
    alpha = x_gate * x_inv
    beta = alpha * x_inv * x_inv * x_mean
    x_markb = x_mark.astype(BF16)
    out_copies = []
    for c in range(CHUNKS):

        def expert_grads(i, _, c=c):
            cols = pl.ds(pl.multiple_of(c * wc + i * TILE, TILE), TILE)
            w = dot(x_markb, ghl[:, cols])
            recv[:, cols] = (alpha * w - beta * xrows[:, cols].astype(F32)).astype(BF16)
            return 0

        lax.fori_loop(0, wc // TILE, expert_grads, 0)
        cols = pl.ds(c * wc, wc)
        copy = pltpu.make_async_copy(recv.at[:, cols], eg_hbm.at[:, cols], out_sem.at[c])
        copy.start()
        out_copies.append(copy)

    for copy in g_copies:
        copy.wait_recv()
    rg_out[...] = agb[...]
    for copy in a_copies + z_copies + e_copies + b_copies + [c_copy] + r_copies + x_copies + g_copies:
        copy.wait_send()
    tg_copy.wait()
    for copy in out_copies:
        copy.wait()


def shards(n_dp, n_ep, tokens, routes, positives, expert_out, router, norm_gain, loss_scale):
    rows, width = tokens.shape
    experts, cap = expert_out.shape[2], expert_out.shape[3]
    slots = experts * cap
    ng = PAIR_DEV * n_ep
    pairs = PAIR_DEV * n_dp * n_ep
    wc, wr = width // CHUNKS, width // n_dp
    dma = pltpu.SemaphoreType.DMA
    vmem = pl.BlockSpec(memory_space=pltpu.VMEM)
    smem = pl.BlockSpec(memory_space=pltpu.SMEM)
    hbm = pl.BlockSpec(memory_space=pl.ANY)
    router_t = jnp.pad(router.T, ((0, 16 - experts), (0, 0)))
    token_grad, expert_grad, router_grad, loss = pl.pallas_call(
        functools.partial(kernel, n_dp, n_ep, experts, cap),
        name="infonce_step",
        out_shape=(
            jax.ShapeDtypeStruct((rows, width), BF16),
            jax.ShapeDtypeStruct((slots, width), BF16),
            jax.ShapeDtypeStruct((n_dp, 8, wr), F32),
            jax.ShapeDtypeStruct((8, 128), F32),
        ),
        in_specs=[hbm, vmem, smem, hbm, vmem, vmem, smem],
        out_specs=(hbm, hbm, vmem, vmem),
        scratch_shapes=[
            pltpu.VMEM((rows, width), BF16),
            pltpu.VMEM((slots, width), BF16),
            pltpu.VMEM((2 * rows, width), BF16),
            pltpu.VMEM((rows, width), F32),
            pltpu.VMEM((rows, 128), F32),
            pltpu.VMEM((2, rows, 128), F32),
            pltpu.VMEM((2 * rows, slots), BF16),
            pltpu.VMEM((2, slots, rows), BF16),
            pltpu.VMEM((slots, width + 128), BF16),
            pltpu.VMEM((slots, width + 128), BF16),
            pltpu.VMEM((16, wc + 128), F32),
            pltpu.VMEM((n_dp * n_ep * 16, wc + 128), BF16),
            pltpu.VMEM((2 * pairs, width), BF16),
            pltpu.VMEM((4 * ng, width), BF16),
            pltpu.VMEM((rows, width), BF16),
            pltpu.VMEM((n_dp, 8, wr), F32),
            pltpu.VMEM((n_dp, 8, wr), F32),
            pltpu.VMEM((n_ep, 8, wr), F32),
            pltpu.VMEM((n_dp, 8, wr), F32),
            dma((1,)),
            dma((2,)),
            dma((CHUNKS, n_ep - 1)),
            dma((CHUNKS, n_ep - 1)),
            dma((n_dp // 2 - 1,)),
            dma((n_dp // 2 - 1,)),
            dma((n_ep - 1,)),
            dma((n_ep - 1,)),
            dma((1,)),
            dma((1,)),
            dma((CHUNKS, n_ep - 1)),
            dma((CHUNKS, n_ep - 1)),
            dma((n_dp - 1,)),
            dma((n_dp - 1,)),
            dma((n_ep - 1,)),
            dma((n_ep - 1,)),
            dma((n_dp - 1,)),
            dma((n_dp - 1,)),
            dma((CHUNKS + 1,)),
        ],
        compiler_params=pltpu.CompilerParams(
            collective_id=0, has_side_effects=True, vmem_limit_bytes=58 * 1024 * 1024
        ),
    )(
        tokens,
        routes,
        positives,
        expert_out.reshape(slots, width),
        router_t,
        norm_gain.reshape(1, width),
        loss_scale.reshape(1),
    )
    router_grad = jnp.transpose(router_grad, (0, 2, 1)).reshape(width, 8)[:, :experts]
    return (token_grad, expert_grad.reshape(expert_out.shape), router_grad, loss[0, 0])


def solution(mesh):
    placed = (
        P(("dp", "expert"), None),
        P(("dp", "expert"), None),
        P(("dp", "expert")),
        P("dp", "expert", None, None, None),
        P(),
        P(),
        P(),
    )
    return jax.shard_map(
        functools.partial(shards, mesh.shape["dp"], mesh.shape["expert"]),
        mesh=mesh,
        in_specs=placed,
        out_specs=(P(("dp", "expert"), None), P("dp", "expert", None, None, None), P(), P()),
        check_vma=False,
    )
```

```python
import functools
import math

import jax
import jax.numpy as jnp
from jax import lax
from jax.experimental import pallas as pl
from jax.experimental.pallas import tpu as pltpu
from jax.sharding import PartitionSpec as P

PAIR_DEV = 2
SEQ = 48
NORM_EPS = 1e-05
CHUNKS = 4
TILE = 512
MESH = pl.DeviceIdType.MESH
BF16, F32, I32 = jnp.bfloat16, jnp.float32, jnp.int32
NT = (((1,), (1,)), ((), ()))


def iota(shape, dim):
    return lax.broadcasted_iota(I32, shape, dim)


def dot(a, b):
    return jnp.dot(a, b, preferred_element_type=F32)


def dot_nt(a, b):
    return lax.dot_general(a, b, NT, preferred_element_type=F32)


def lane_sum(x):
    return jnp.sum(x, axis=1, keepdims=True)


def fold(x):
    total = x[:, :128]
    for i in range(1, x.shape[1] // 128):
        total = total + x[:, i * 128 : (i + 1) * 128]
    return total


def split3(x):
    hi = x.astype(BF16).astype(F32)
    mid = (x - hi).astype(BF16).astype(F32)
    return hi, mid, x - hi - mid


def log2(n):
    assert n & (n - 1) == 0
    return n.bit_length() - 1


def kernel(
    n_dp, n_ep, experts, cap,
    tok_hbm, routes_ref, pos_ref, eo_hbm, router_ref, gain_ref, scale_ref,
    tg_hbm, xr_hbm, rg_out, loss_ref, ghl_out, ab_ref,
    tok, recv, feat, summed, sq, sf, pick, pick_t, back, xrows, pay, gath, qr, ghl, tgb, rpart, rsb, exb, agb,
    tok_sem, own_sem, a_send, a_recv, z_send, z_recv, e_send, e_recv, c_send, c_recv,
    b_send, b_recv, r_send, r_recv, x_send, x_recv, g_send, g_recv, out_sem,
):
    d = lax.axis_index("dp")
    e = lax.axis_index("expert")
    rows, width = tok.shape
    slots = experts * cap
    n_z = n_dp // 2
    core, z = lax.rem(d, 2), d // 2
    pairs = PAIR_DEV * n_dp * n_ep
    wc = width // CHUNKS
    wr = width // n_dp
    ng = PAIR_DEV * n_ep
    score_scale = 4.0 / math.sqrt(width)

    def dp_peer(o):
        return lax.rem(d + o, n_dp)

    def ep_peer(o):
        return lax.rem(e + o, n_ep)

    barrier = pltpu.get_barrier_semaphore()
    for o in range(1, n_dp):
        pl.semaphore_signal(barrier, inc=1, device_id=(dp_peer(o), e), device_id_type=MESH)
    for o in range(1, n_ep):
        pl.semaphore_signal(barrier, inc=1, device_id=(d, ep_peer(o)), device_id_type=MESH)

    tok_copy = pltpu.make_async_copy(tok_hbm, tok, tok_sem.at[0])
    tok_copy.start()

    def ep_rows(i):
        return pl.ds(pl.multiple_of(i * cap, cap), cap)

    own_copy = pltpu.make_async_copy(eo_hbm.at[ep_rows(e)], recv.at[ep_rows(e)], own_sem.at[0])
    own_copy.start()
    pl.semaphore_wait(barrier, n_dp - 1 + n_ep - 1)

    a_copies = []
    for c in range(CHUNKS):
        cols = pl.ds(c * wc, wc)
        for o in range(1, n_ep):
            copy = pltpu.make_async_remote_copy(
                src_ref=eo_hbm.at[ep_rows(ep_peer(o)), cols],
                dst_ref=recv.at[ep_rows(e), cols],
                send_sem=a_send.at[c, o - 1],
                recv_sem=a_recv.at[c, o - 1],
                device_id=(d, ep_peer(o)),
                device_id_type=MESH,
            )
            copy.start()
            a_copies.append(copy)

    tok_copy.wait()
    logits = dot_nt(tok[...], router_ref[...])
    route = [routes_ref[:, 0:1], routes_ref[:, 1:2]]
    lane_e = iota((rows, 128), 1)
    lane_l = iota(logits.shape, 1)
    chosen = [lane_sum(jnp.where(lane_l == r, logits, 0.0)) for r in route]
    highest = jnp.maximum(chosen[0], chosen[1])
    expo = [jnp.exp(x - highest) for x in chosen]
    gate = [x / (expo[0] + expo[1]) for x in expo]
    hits = jnp.where((lane_e == route[0]) | (lane_e == route[1]), 1.0, 0.0).astype(BF16)
    lower = jnp.where(iota((rows, rows), 1) < iota((rows, rows), 0), 1.0, 0.0).astype(BF16)
    before = dot(lower, hits)
    column = iota((rows, slots), 1).astype(F32)
    for k in range(2):
        rank = lane_sum(jnp.where(lane_e == route[k], before, 0.0))
        slot = route[k].astype(F32) * float(cap) + rank
        one = jnp.where(column == slot, 1.0, 0.0)
        pick[k * rows : (k + 1) * rows, :] = one.astype(BF16)
        pick_t[k, :, :] = jnp.transpose(one).astype(BF16)

    sq[...] = jnp.zeros_like(sq)
    sf[...] = jnp.zeros_like(sf)
    own_copy.wait()
    for c in range(CHUNKS):
        for o in range(1, n_ep):
            a_copies[c * (n_ep - 1) + o - 1].wait_recv()

        def forward(i, _, c=c):
            cols = pl.ds(pl.multiple_of(c * wc + i * TILE, TILE), TILE)
            got = dot(pick[...], recv[:, cols])
            feat[:, cols] = got.astype(BF16)
            f0, f1 = got[:rows], got[rows:]
            s = tok[:, cols].astype(F32) + gate[0] * f0 + gate[1] * f1
            summed[:, cols] = s
            sq[...] += fold(s * s)
            sf[0, :, :] += fold(s * f0)
            sf[1, :, :] += fold(s * f1)
            return 0

        lax.fori_loop(0, wc // TILE, forward, 0)

    inverse = lax.rsqrt(lane_sum(sq[...]) * (1.0 / width) + NORM_EPS)
    for c in range(CHUNKS):
        for i in range(wc // TILE):
            cols = slice(c * wc + i * TILE, c * wc + (i + 1) * TILE)
            normed = summed[:, cols] * inverse * gain_ref[:, cols]
            for q in range(2 * PAIR_DEV):
                pay[c * 4 + q : c * 4 + q + 1, i * TILE : (i + 1) * TILE] = jnp.sum(
                    normed[q * SEQ : (q + 1) * SEQ], axis=0, keepdims=True
                ) * (1.0 / SEQ)
    tag_row, tag_lane = iota((16, 128), 0), iota((16, 128), 1)
    tags = jnp.zeros((16, 128), F32)
    for q in range(PAIR_DEV):
        p = pos_ref[q]
        high = jnp.right_shift(p, 4).astype(F32)
        low = jnp.bitwise_and(p, 15).astype(F32)
        tags = jnp.where((tag_row == q) & (tag_lane == 0), high, tags)
        tags = jnp.where((tag_row == q) & (tag_lane == 1), low, tags)
    pay[:, wc:] = tags

    def block(first, count):
        return pl.ds(pl.multiple_of(first * 16, 16), count * 16)

    mine = (core * n_ep + e) * n_z + z
    gath[block(mine, 1), :] = pay[...].astype(BF16)
    z_copies = []
    for o in range(1, n_z):
        copy = pltpu.make_async_remote_copy(
            src_ref=gath.at[block(mine, 1)],
            dst_ref=gath.at[block(mine, 1)],
            send_sem=z_send.at[o - 1],
            recv_sem=z_recv.at[o - 1],
            device_id=(dp_peer(2 * o), e),
            device_id_type=MESH,
        )
        copy.start()
        z_copies.append(copy)

    seq_of = iota((rows, 1), 0) // SEQ
    code = jnp.where(seq_of < PAIR_DEV, e * PAIR_DEV + seq_of, ng + e * PAIR_DEV + seq_of - PAIR_DEV)
    inv3 = split3(inverse)
    notes = jnp.zeros((slots, 128), F32)
    for k in range(2):
        values = list(split3(gate[k])) + list(inv3) + [code.astype(F32)]
        note = jnp.zeros((rows, 128), F32)
        for i, v in enumerate(values):
            note = jnp.where(lane_e == i, v, note)
        notes = notes + dot(pick_t[k], note.astype(BF16))
    back[:, width:] = notes.astype(BF16)

    def place(i, _):
        cols = pl.ds(pl.multiple_of(i * TILE, TILE), TILE)
        both = pick_t[0] + pick_t[1]
        back[:, cols] = dot(both, summed[:, cols].astype(BF16)).astype(BF16)
        return 0

    lax.fori_loop(0, width // TILE, place, 0)

    for copy in z_copies:
        copy.wait_recv()
    line = (core * n_ep + e) * n_z
    e_copies = []
    for o in range(1, n_ep):
        copy = pltpu.make_async_remote_copy(
            src_ref=gath.at[block(line, n_z)],
            dst_ref=gath.at[block(line, n_z)],
            send_sem=e_send.at[o - 1],
            recv_sem=e_recv.at[o - 1],
            device_id=(d, ep_peer(o)),
            device_id_type=MESH,
        )
        copy.start()
        e_copies.append(copy)
    back_own = pltpu.make_async_copy(back.at[ep_rows(e)], xrows.at[ep_rows(e)], own_sem.at[1])
    back_own.start()
    b_copies = []
    for c in range(CHUNKS):
        cols = pl.ds(c * wc, wc + (128 if c == CHUNKS - 1 else 0))
        for o in range(1, n_ep):
            copy = pltpu.make_async_remote_copy(
                src_ref=back.at[ep_rows(ep_peer(o)), cols],
                dst_ref=xrows.at[ep_rows(e), cols],
                send_sem=b_send.at[c, o - 1],
                recv_sem=b_recv.at[c, o - 1],
                device_id=(d, ep_peer(o)),
                device_id_type=MESH,
            )
            copy.start()
            b_copies.append(copy)
    for copy in e_copies:
        copy.wait_recv()
    half = core * n_ep * n_z
    c_copy = pltpu.make_async_remote_copy(
        src_ref=gath.at[block(half, n_ep * n_z)],
        dst_ref=gath.at[block(half, n_ep * n_z)],
        send_sem=c_send.at[0],
        recv_sem=c_recv.at[0],
        device_id=(d + 1 - 2 * core, e),
        device_id_type=MESH,
    )
    c_copy.start()
    c_copy.wait_recv()

    total = n_dp * n_ep * 16
    which = iota((2 * pairs, total), 0)
    source = iota((2 * pairs, total), 1)
    pair = jnp.bitwise_and(which, pairs - 1)
    is_record = jnp.right_shift(which, log2(pairs))
    blk = jnp.right_shift(pair, log2(PAIR_DEV))
    of_e = jnp.bitwise_and(blk, n_ep - 1)
    of_d = jnp.right_shift(blk, log2(n_ep))
    place_of = (jnp.bitwise_and(of_d, 1) * n_ep + of_e) * n_z + jnp.right_shift(of_d, 1)
    start = place_of * 16 + is_record * PAIR_DEV + jnp.bitwise_and(pair, PAIR_DEV - 1)
    for c in range(CHUNKS):
        take = jnp.where(source == start + c * 4, 1.0, 0.0).astype(BF16)
        if c == 0:
            tag = dot(take[:pairs], gath[:, wc:])
            positive = tag[:, 0:1] * 16.0 + tag[:, 1:2]
        qr[:, c * wc : (c + 1) * wc] = dot(take, gath[:, :wc]).astype(BF16)
    scores = dot_nt(qr[:pairs], qr[pairs:]) * score_scale
    top = jnp.max(scores, axis=1, keepdims=True)
    log_total = top + jnp.log(lane_sum(jnp.exp(scores - top)))
    is_positive = iota((pairs, pairs), 1).astype(F32) == positive
    positive_score = lane_sum(jnp.where(is_positive, scores, 0.0))
    loss = jnp.sum(log_total - positive_score, axis=0, keepdims=True) * (1.0 / pairs)
    loss_ref[...] = jnp.broadcast_to(loss, loss_ref.shape)
    score_grad = (
        (jnp.exp(scores - log_total) - jnp.where(is_positive, 1.0, 0.0)) * (scale_ref[0] * (1.0 / pairs))
    ).astype(BF16)
    group_shape = (max(16, ng), pairs)
    group = jnp.where(iota(group_shape, 1) == iota(group_shape, 0) + d * ng, 1.0, 0.0).astype(BF16)
    grad_q = dot(group, score_grad).astype(BF16)
    grad_r = dot_nt(group, score_grad).astype(BF16)

    def pooled_grads(i, _):
        cols = pl.ds(pl.multiple_of(i * TILE, TILE), TILE)
        gq = dot(grad_q, qr[pairs:, cols])[:ng]
        gr = dot(grad_r, qr[:pairs, cols])[:ng]
        g = jnp.concatenate([gq, gr], axis=0) * (score_scale / SEQ) * gain_ref[:, cols]
        hi = g.astype(BF16)
        ghl[: 2 * ng, cols] = hi
        ghl[2 * ng :, cols] = (g - hi.astype(F32)).astype(BF16)
        return 0

    lax.fori_loop(0, width // TILE, pooled_grads, 0)

    lane_g = iota((rows, 4 * ng), 1)
    mark = jnp.where((lane_g == code) | (lane_g == code + 2 * ng), 1.0, 0.0)
    own = lane_sum(mark * dot_nt(tok[...], ghl[...]))
    along = dot_nt(feat[...], ghl[...])
    a0, a1 = lane_sum(mark * along[:rows]), lane_sum(mark * along[rows:])
    mean_ws = (own + gate[0] * a0 + gate[1] * a1) * (1.0 / width)
    coef = inverse * inverse * inverse * mean_ws
    gg0 = inverse * a0 - coef * lane_sum(sf[0])
    gg1 = inverse * a1 - coef * lane_sum(sf[1])
    gg = gate[0] * gg0 + gate[1] * gg1
    grad_logits = jnp.where(lane_e == route[0], gate[0] * (gg0 - gg), 0.0) + jnp.where(
        lane_e == route[1], gate[1] * (gg1 - gg), 0.0
    )
    gl = grad_logits[:, :16].astype(BF16)
    gl_t = jnp.transpose(grad_logits)[:16].astype(BF16)
    for i in range(n_dp):
        rpart[i, :, :] = dot(gl_t, tok[:, i * wr : (i + 1) * wr])[:8]
    rsb[d] = rpart[d]
    r_copies = []
    for o in range(1, n_dp):
        copy = pltpu.make_async_remote_copy(
            src_ref=rpart.at[dp_peer(o)],
            dst_ref=rsb.at[d],
            send_sem=r_send.at[o - 1],
            recv_sem=r_recv.at[o - 1],
            device_id=(dp_peer(o), e),
            device_id_type=MESH,
        )
        copy.start()
        r_copies.append(copy)
    markb = mark.astype(BF16)

    def token_grads(i, _):
        cols = pl.ds(pl.multiple_of(i * TILE, TILE), TILE)
        w = dot(markb, ghl[:, cols])
        through = dot(gl, router_ref[:, cols])
        tgb[:, cols] = (inverse * w - coef * summed[:, cols] + through).astype(BF16)
        return 0

    lax.fori_loop(0, width // TILE, token_grads, 0)
    tg_copy = pltpu.make_async_copy(tgb, tg_hbm, out_sem.at[CHUNKS])
    tg_copy.start()

    for copy in r_copies:
        copy.wait_recv()
    part = rsb[0]
    for i in range(1, n_dp):
        part = part + rsb[i]
    exb[e] = part
    x_copies = []
    for o in range(1, n_ep):
        copy = pltpu.make_async_remote_copy(
            src_ref=exb.at[e],
            dst_ref=exb.at[e],
            send_sem=x_send.at[o - 1],
            recv_sem=x_recv.at[o - 1],
            device_id=(d, ep_peer(o)),
            device_id_type=MESH,
        )
        copy.start()
        x_copies.append(copy)

    back_own.wait()
    ghl_out[...] = ghl[...]
    out_copies = []
    dots = jnp.zeros((slots, 4 * ng), F32)
    for c in range(CHUNKS):
        for o in range(1, n_ep):
            b_copies[c * (n_ep - 1) + o - 1].wait_recv()
        cols = pl.ds(c * wc, wc)
        copy = pltpu.make_async_copy(xrows.at[:, cols], xr_hbm.at[:, cols], out_sem.at[c])
        copy.start()
        out_copies.append(copy)
        dots = dots + dot_nt(xrows[:, c * wc : (c + 1) * wc], ghl[:, c * wc : (c + 1) * wc])

    for copy in x_copies:
        copy.wait_recv()
    part = exb[0]
    for i in range(1, n_ep):
        part = part + exb[i]
    agb[d] = part
    g_copies = []
    for o in range(1, n_dp):
        copy = pltpu.make_async_remote_copy(
            src_ref=agb.at[d],
            dst_ref=agb.at[d],
            send_sem=g_send.at[o - 1],
            recv_sem=g_recv.at[o - 1],
            device_id=(dp_peer(o), e),
            device_id_type=MESH,
        )
        copy.start()
        g_copies.append(copy)

    note = xrows[:, width:].astype(F32)
    x_gate = note[:, 0:1] + note[:, 1:2] + note[:, 2:3]
    x_inv = note[:, 3:4] + note[:, 4:5] + note[:, 5:6]
    x_code = note[:, 6:7]
    lane_x = iota((slots, 4 * ng), 1).astype(F32)
    x_mark = jnp.where((lane_x == x_code) | (lane_x == x_code + float(2 * ng)), 1.0, 0.0)
    x_mean = lane_sum(x_mark * dots) * (1.0 / width)
    alpha = x_gate * x_inv
    beta = alpha * x_inv * x_inv * x_mean
    lane_s = iota((slots, 128), 1)
    ab = jnp.where(lane_s == 0, alpha, 0.0)
    ab = jnp.where(lane_s == 1, beta, ab)
    ab_ref[...] = jnp.where(lane_s == 2, x_code, ab)

    for copy in g_copies:
        copy.wait_recv()
    rg_out[...] = agb[...]
    for copy in a_copies + z_copies + e_copies + b_copies + [c_copy] + r_copies + x_copies + g_copies:
        copy.wait_send()
    tg_copy.wait()
    for copy in out_copies:
        copy.wait()


def finish(tg_in, x_ref, ghl_ref, ab_ref, tg_ref, eg_ref):
    tg_ref[...] = tg_in[...]
    slots, marks = x_ref.shape[0], ghl_ref.shape[0]
    alpha, beta, code = ab_ref[:, 0:1], ab_ref[:, 1:2], ab_ref[:, 2:3]
    lane = iota((slots, marks), 1).astype(F32)
    mark = jnp.where((lane == code) | (lane == code + float(marks // 2)), 1.0, 0.0).astype(BF16)
    w = dot(mark, ghl_ref[...])
    eg_ref[...] = (alpha * w - beta * x_ref[...].astype(F32)).astype(BF16)


def shards(n_dp, n_ep, tokens, routes, positives, expert_out, router, norm_gain, loss_scale):
    rows, width = tokens.shape
    experts, cap = expert_out.shape[2], expert_out.shape[3]
    slots = experts * cap
    ng = PAIR_DEV * n_ep
    pairs = PAIR_DEV * n_dp * n_ep
    wc, wr = width // CHUNKS, width // n_dp
    dma = pltpu.SemaphoreType.DMA
    vmem = pl.BlockSpec(memory_space=pltpu.VMEM)
    smem = pl.BlockSpec(memory_space=pltpu.SMEM)
    hbm = pl.BlockSpec(memory_space=pl.ANY)
    router_t = jnp.pad(router.T, ((0, 16 - experts), (0, 0)))
    tg_rows, x_rows, router_grad, loss, pooled_hl, factors = pl.pallas_call(
        functools.partial(kernel, n_dp, n_ep, experts, cap),
        name="infonce_step",
        out_shape=(
            jax.ShapeDtypeStruct((rows, width), BF16),
            jax.ShapeDtypeStruct((slots, width), BF16),
            jax.ShapeDtypeStruct((n_dp, 8, wr), F32),
            jax.ShapeDtypeStruct((8, 128), F32),
            jax.ShapeDtypeStruct((4 * ng, width), BF16),
            jax.ShapeDtypeStruct((slots, 128), F32),
        ),
        in_specs=[hbm, vmem, smem, hbm, vmem, vmem, smem],
        out_specs=(hbm, hbm, vmem, vmem, vmem, vmem),
        scratch_shapes=[
            pltpu.VMEM((rows, width), BF16),
            pltpu.VMEM((slots, width), BF16),
            pltpu.VMEM((2 * rows, width), BF16),
            pltpu.VMEM((rows, width), F32),
            pltpu.VMEM((rows, 128), F32),
            pltpu.VMEM((2, rows, 128), F32),
            pltpu.VMEM((2 * rows, slots), BF16),
            pltpu.VMEM((2, slots, rows), BF16),
            pltpu.VMEM((slots, width + 128), BF16),
            pltpu.VMEM((slots, width + 128), BF16),
            pltpu.VMEM((16, wc + 128), F32),
            pltpu.VMEM((n_dp * n_ep * 16, wc + 128), BF16),
            pltpu.VMEM((2 * pairs, width), BF16),
            pltpu.VMEM((4 * ng, width), BF16),
            pltpu.VMEM((rows, width), BF16),
            pltpu.VMEM((n_dp, 8, wr), F32),
            pltpu.VMEM((n_dp, 8, wr), F32),
            pltpu.VMEM((n_ep, 8, wr), F32),
            pltpu.VMEM((n_dp, 8, wr), F32),
            dma((1,)),
            dma((2,)),
            dma((CHUNKS, n_ep - 1)),
            dma((CHUNKS, n_ep - 1)),
            dma((n_dp // 2 - 1,)),
            dma((n_dp // 2 - 1,)),
            dma((n_ep - 1,)),
            dma((n_ep - 1,)),
            dma((1,)),
            dma((1,)),
            dma((CHUNKS, n_ep - 1)),
            dma((CHUNKS, n_ep - 1)),
            dma((n_dp - 1,)),
            dma((n_dp - 1,)),
            dma((n_ep - 1,)),
            dma((n_ep - 1,)),
            dma((n_dp - 1,)),
            dma((n_dp - 1,)),
            dma((CHUNKS + 1,)),
        ],
        compiler_params=pltpu.CompilerParams(
            collective_id=0, has_side_effects=True, vmem_limit_bytes=58 * 1024 * 1024
        ),
    )(
        tokens,
        routes,
        positives,
        expert_out.reshape(slots, width),
        router_t,
        norm_gain.reshape(1, width),
        loss_scale.reshape(1),
    )
    tile = min(1024, width)
    by_cols = lambda n: pl.BlockSpec((n, tile), lambda i: (0, i))
    token_grad, expert_grad = pl.pallas_call(
        finish,
        name="finish_grads",
        grid=(width // tile,),
        out_shape=(
            jax.ShapeDtypeStruct((rows, width), BF16),
            jax.ShapeDtypeStruct((slots, width), BF16),
        ),
        in_specs=[
            by_cols(rows),
            by_cols(slots),
            by_cols(4 * ng),
            pl.BlockSpec((slots, 128), lambda i: (0, 0)),
        ],
        out_specs=(by_cols(rows), by_cols(slots)),
        compiler_params=pltpu.CompilerParams(vmem_limit_bytes=32 * 1024 * 1024),
    )(tg_rows, x_rows, pooled_hl, factors)
    router_grad = jnp.transpose(router_grad, (0, 2, 1)).reshape(width, 8)[:, :experts]
    return (token_grad, expert_grad.reshape(expert_out.shape), router_grad, loss[0, 0])


def solution(mesh):
    placed = (
        P(("dp", "expert"), None),
        P(("dp", "expert"), None),
        P(("dp", "expert")),
        P("dp", "expert", None, None, None),
        P(),
        P(),
        P(),
    )
    return jax.shard_map(
        functools.partial(shards, mesh.shape["dp"], mesh.shape["expert"]),
        mesh=mesh,
        in_specs=placed,
        out_specs=(P(("dp", "expert"), None), P("dp", "expert", None, None, None), P(), P()),
        check_vma=False,
    )
```
